256 devices in a mesh: row: 16 (over x, z_lo), col: 16 (over y, z_hi, core).
Axes of the slice: x: 4, y: 4, z: 8 (z_hi: 2, z_lo: 4; z = z_hi * 4 + z_lo), core: 2. Of those that a mesh axis runs over, the one named last changes fastest.
Arguments:
- inputs: bfloat16 [896, 8192], P('col', 'row'), may hold values from -6 to 6
- out_grad: bfloat16 [896, 8192], P('col', 'row'), may hold values from -1.59375 to 1.59375
- gate_weight: bfloat16 [8192, 28672], P('row', 'col'), may hold values from -0.0625 to 0.0625
- up_weight: bfloat16 [8192, 28672], P('row', 'col'), may hold values from -0.0625 to 0.0625
- down_weight: bfloat16 [28672, 8192], P('col', 'row'), may hold values from -0.03125 to 0.03125
Outputs:
- input_grad: bfloat16 [896, 8192], P('col', 'row')
- gate_grad: bfloat16 [8192, 28672], P('row', 'col')
- up_grad: bfloat16 [8192, 28672], P('row', 'col')
- down_grad: bfloat16 [28672, 8192], P('col', 'row')
The draws below stay inside these ranges and needn't reach their ends.
All inputs are finite; a program needn't handle non-finite values.
Results may differ from the reference program's by a relative error of at most 0.005.
Values may be sent and summed in bfloat16 or wider, within the bound.
No kernel may reach another device: no remote copies, remote signals or barrier semaphores. Data moves between devices by JAX's collectives and lax.ppermute only.
A program may use at most 128 MiB of HBM per device.

```python
import jax
import jax.numpy as jnp
from jax import lax

D = 8192
FF = 28672
TOKENS = 896


def shard_levels(own_key, shape, cuts, low, largest):
    factor_of, own = 1.0, jax.random.fold_in(own_key, 6)
    for dim, blocks in cuts:
        heights = jnp.exp(jax.random.uniform(jax.random.fold_in(own, dim), (blocks,), jnp.float32, low / len(cuts), largest / len(cuts)))
        factor_of = factor_of * jnp.repeat(heights, shape[dim] // blocks).reshape([-1 if axis == dim else 1 for axis in range(len(shape))])
    return factor_of


def gaussian(stream_key, dims, deviation, bound, pieces=(), held_as=jnp.bfloat16):
    level = shard_levels(stream_key, dims, pieces, -0.22, 0.18) if pieces else 1.0
    array = jax.random.normal(stream_key, dims, jnp.float32) * deviation * level
    return jnp.minimum(jnp.maximum(array, -bound), bound).astype(held_as)


def setup_inputs(seed: int = 0) -> dict:
    key_list = jax.random.split(jax.random.key(seed), 6)
    inputs = gaussian(key_list[0], (TOKENS, D), 1.0, 6.0, ((0, 16), (1, 16)))
    out_grad = gaussian(key_list[1], (TOKENS, D), 0.2, 1.59375, ((0, 16), (1, 16)))
    gate_weight = gaussian(key_list[2], (D, FF), D ** -0.5, 0.0625, ((0, 16), (1, 16)))
    up_weight = gaussian(key_list[3], (D, FF), D ** -0.5, 0.0625, ((0, 16), (1, 16)))
    down_weight = gaussian(key_list[4], (FF, D), FF ** -0.5, 0.03125, ((0, 16), (1, 16)))
    return {"inputs": inputs, "out_grad": out_grad, "gate_weight": gate_weight, "up_weight": up_weight, "down_weight": down_weight}


def reference(inputs, out_grad, gate_weight, up_weight, down_weight):
    gate = jnp.dot(inputs, gate_weight, preferred_element_type=jnp.float32)
    up = jnp.dot(inputs, up_weight, preferred_element_type=jnp.float32)
    back = lax.dot_general(out_grad, down_weight, (((1,), (1,)), ((), ())), preferred_element_type=jnp.float32)
    sig = jax.nn.sigmoid(gate)
    silu = gate * sig
    hidden = (silu * up).astype(jnp.bfloat16)
    d_up = (back * silu).astype(jnp.bfloat16)
    d_gate = (back * up * sig * (1.0 + gate * (1.0 - sig))).astype(jnp.bfloat16)
    contract_rows = (((0,), (0,)), ((), ()))
    gate_grad = lax.dot_general(inputs, d_gate, contract_rows, preferred_element_type=jnp.float32)
    up_grad = lax.dot_general(inputs, d_up, contract_rows, preferred_element_type=jnp.float32)
    down_grad = lax.dot_general(hidden, out_grad, contract_rows, preferred_element_type=jnp.float32)
    contract_cols = (((1,), (1,)), ((), ()))
    input_grad = lax.dot_general(d_gate, gate_weight, contract_cols, preferred_element_type=jnp.float32)
    input_grad = input_grad + lax.dot_general(d_up, up_weight, contract_cols, preferred_element_type=jnp.float32)
    return (input_grad.astype(jnp.bfloat16), gate_grad.astype(jnp.bfloat16),
            up_grad.astype(jnp.bfloat16), down_grad.astype(jnp.bfloat16))
```

```python
import jax
import jax.numpy as jnp
from jax import lax
from jax.sharding import Mesh, PartitionSpec as P

BF16, F16, F32 = jnp.bfloat16, jnp.float16, jnp.float32
DIMS = {
    "A": ("x", 4, 1), "B": ("x", 4, 3), "C": ("zl", 4, 1), "D": ("zl", 4, 2),
    "E": ("y", 4, 1), "F": ("y", 4, 3), "G": ("zh", 2, 1), "H": ("c", 2, 1),
}
ROW, COL = "ABCD", "HFEG"
CHUNKS = ((384, 'ACB', 'BAC'), (384, 'BAC', 'CAB'), (384, 'BAC', 'CAB'), (256, 'BAC', 'ABC'), (384, 'CAB', 'BCA'))
ORDER = (1, 2, 0, 3, 4, 1, 0, 4, 1, 2, 0, 4, 1, 3, 2, 0, 4, 1, 3, 2, 0, 1, 3, 4, 0, 2, 1, 4, 3, 2, 0, 3, 4, 2, 3)
LAG = 3
contract_rows = (((0,), (0,)), ((), ()))
contract_cols = (((1,), (1,)), ((), ()))


def swap(value, dim):
    axis, size, flip = DIMS[dim]
    return lax.ppermute(value, axis, [(i, i ^ flip) for i in range(size)])


def take(value, names, dim, index):
    return lax.index_in_dim(value, index, names.index(dim), keepdims=False)


def pick(value, names, dim, index):
    return lax.dynamic_index_in_dim(value, index, names.index(dim), keepdims=False)


def powers_for(bound):
    up, down = jnp.ones_like(bound), jnp.ones_like(bound)
    for power in (30, 15, 8, 4, 2, 1):
        fits = bound * 2.0**power <= 2.0**15
        bound = jnp.where(fits, bound * 2.0**power, bound)
        up = jnp.where(fits, up * 2.0**power, up)
        down = jnp.where(fits, down * 0.5**power, down)
    return up, down


def local_backward(total, size):
    gate, up, back = total[:, :size], total[:, size : 2 * size], total[:, 2 * size :]
    sig = jax.nn.sigmoid(gate)
    silu = gate * sig
    hidden = (silu * up).astype(BF16)
    d_up = (back * silu).astype(BF16)
    d_gate = (back * up * sig * (1.0 + gate * (1.0 - sig))).astype(BF16)
    return jnp.concatenate([d_gate, d_up, hidden], axis=1)


def merge(pair, order):
    names = "".join(n for n in ROW if n in order)
    return jnp.stack(pair, axis=names.index(order[-1]))


def on_device(inputs, out_grad, gate_weight, up_weight, down_weight):
    rows, width = inputs.shape
    x, zl = lax.axis_index("x"), lax.axis_index("zl")
    bit = {"H": (x & 1) ^ (x >> 1), "F": x >> 1, "E": zl & 1, "G": zl >> 1}

    def gather(value, order, names):
        for dim in order:
            names = "".join(n for n in COL if n in names or n == dim)
            other = swap(value, dim)
            mine = bit[dim] == 0
            value = jnp.stack([jnp.where(mine, value, other), jnp.where(mine, other, value)], axis=names.index(dim))
        return value

    both = gather(jnp.concatenate([inputs, out_grad], axis=1), "G", "")
    x_cols = gather(both[..., :width], "EFH", "G")
    g_cols = gather(both[..., width:], "FEH", "G")
    x_flat, g_flat = (v.reshape(16 * rows, width) for v in (x_cols, g_cols))
    x_turned = x_flat.T
    def forward(cols, first, index, start, size):
        xh, gh = (take(v, ROW, first, index).reshape(8 * rows, width) for v in cols)
        gate = jnp.dot(xh, gate_weight[:, start : start + size], preferred_element_type=F32)
        up = jnp.dot(xh, up_weight[:, start : start + size], preferred_element_type=F32)
        back = lax.dot_general(gh, down_weight[start : start + size], contract_cols, preferred_element_type=F32)
        return jnp.concatenate([gate, up, back], axis=1).reshape(2, 2, 2, rows, 3 * size)

    starts = [sum(c[0] for c in CHUNKS[:i]) for i in range(len(CHUNKS))]
    state = [None] * len(CHUNKS)
    step = [0] * len(CHUNKS)
    last = None
    due = {}
    grads = [None] * len(CHUNKS)
    acc_input = 0.0

    def tie(value, *more):
        nonlocal last
        if last is not None:
            value, last, more = lax.optimization_barrier((value, last, more))
        last = value
        return (value, *more) if more else value

    def after(*values):
        nonlocal last
        values, last = lax.optimization_barrier((values, last))
        return values

    def send(value, dim):
        return swap(tie(value.astype(BF16)), dim)

    def send_scaled(value, dim):
        up, down = powers_for(jnp.max(jnp.abs(value), axis=0, keepdims=True))
        down = swap(tie(jnp.broadcast_to(down, (8, down.shape[1])).astype(BF16)), dim)
        return swap(tie((value * up).astype(F16)), dim), down

    def split(value, size):
        return value[:, :size], value[:, size : 2 * size], value[:, 2 * size :]

    def input_products(i):
        size, _, up = CHUNKS[i]
        columns = slice(starts[i], starts[i] + size)
        d_gate, d_up, _ = split(merge(state[i], "D" + up).reshape(16 * rows, 3 * size), size)
        part = lax.dot_general(d_gate, gate_weight[:, columns], contract_cols, preferred_element_type=F32)
        return part + lax.dot_general(d_up, up_weight[:, columns], contract_cols, preferred_element_type=F32)

    def weight_products(i):
        size, _, up = CHUNKS[i]
        d_gate, d_up, hidden = split(merge(state[i], "D" + up).reshape(16 * rows, 3 * size), size)
        return (
            jnp.dot(x_turned, d_gate, preferred_element_type=F32).astype(BF16),
            jnp.dot(x_turned, d_up, preferred_element_type=F32).astype(BF16),
            lax.dot_general(hidden, g_flat, contract_rows, preferred_element_type=F32).astype(BF16),
        )

    for n, i in enumerate(ORDER):
        size, down, up = CHUNKS[i]
        s = step[i]
        names = "".join(n for n in ROW if n not in down[:s])
        if s == 0:
            dim = down[0]
            state[i] = [send(forward((x_cols, g_cols), dim, 1, starts[i], size), dim)]
        elif s < 3:
            dim = down[s]
            state[i][-1], *cols = after(state[i][-1], x_cols, g_cols)
            if s == 1:
                state[i] = [forward(cols, down[0], 0, starts[i], size), *state[i]]
            other = send(sum(take(p, names, dim, 1).astype(F32) for p in state[i]), dim)
            state[i] = [take(p, names, dim, 0) for p in state[i]] + [other]
        elif s == 3:
            state[i][-1], = after(state[i][-1])
            value = sum(p.astype(F32) for p in state[i]).reshape(2 * rows, 3 * size)
            state[i] = (value, *send_scaled(value, "D"))
        else:
            state[i] = (state[i][0], *after(*state[i][1:]))
            if s == 4:
                value, other, down = state[i]
                other = other.astype(F32) * down[:1].astype(F32)
                other = other.reshape(2, rows, 3 * size)[::-1].reshape(2 * rows, 3 * size)
                value = local_backward(value + other, size)
                value = value.reshape(2, rows, 3 * size)
            else:
                value = merge(state[i], "D" + up[: s - 4])
            if due and min(due) <= n:
                j = due.pop(min(due))
                value, acc_input, grads[j] = tie(value, acc_input + input_products(j), weight_products(j))
            else:
                value = tie(value)
            state[i] = (value, swap(value, up[s - 4]))
        step[i] += 1
        if step[i] == 7:
            due[n + LAG] = i

    def scatter(value, order, names):
        for dim in order:
            kept = pick(value, names, dim, bit[dim])
            value = kept + swap(pick(value, names, dim, 1 - bit[dim]), dim)
            names = names.replace(dim, "")
        return value

    for j in due.values():
        acc_input = acc_input + input_products(j)
    acc_input = tie(acc_input.reshape(2, 2, 2, 2, rows, width))
    acc_input = scatter(acc_input, "H", COL)
    left = scatter(acc_input[..., : width // 2], "FE", "FEG")
    right = scatter(acc_input[..., width // 2 :], "EF", "FEG")
    acc_input = scatter(jnp.concatenate([left, right], axis=-1), "G", "G")
    for j in due.values():
        state[j], last = lax.optimization_barrier((state[j], last))
        grads[j] = weight_products(j)
    gate_grads, up_grads, down_grads = zip(*grads)
    return (
        acc_input.astype(BF16),
        jnp.concatenate(gate_grads, axis=1),
        jnp.concatenate(up_grads, axis=1),
        jnp.concatenate(down_grads, axis=0),
    )


def solution(mesh):
    fine = Mesh(mesh.devices.reshape(4, 4, 4, 2, 2), ("x", "zl", "y", "zh", "c"))
    row, col = ("x", "zl"), ("y", "zh", "c")
    in_specs = (P(col, row), P(col, row), P(row, col), P(row, col), P(col, row))
    out_specs = (P(col, row), P(row, col), P(row, col), P(col, row))
    return jax.shard_map(
        on_device, mesh=fine, in_specs=in_specs, out_specs=out_specs, check_vma=False
    )
```

```python
import jax
import jax.numpy as jnp
from jax import lax
from jax.experimental.layout import Layout, with_layout_constraint
from jax.sharding import Mesh, PartitionSpec as P

BF16, F32 = jnp.bfloat16, jnp.float32
DIMS = {
    "P": (("x", 1), ("x", 3)), "Q": (("x", 3), ("zl", 1)), "R": (("zl", 1), ("x", 1)), "D": (("zl", 2),),
    "E": (("y", 1),), "F": (("y", 3),), "G": (("zh", 1),), "H": (("c", 1),),
}
SIZES = {"x": 4, "zl": 4, "y": 4, "zh": 2, "c": 2}
ROW, COL = "PQRD", "HFEG"
CHUNKS = ((512, 'QRP', 'PRQ'), (384, 'QPR', 'PQR'), (384, 'PRQ', 'PRQ'), (512, 'PRQ', 'QRP'))
ORDER = (2, 3, 0, 1, 2, 3, 2, 0, 3, 1, 2, 0, 3, 1, 2, 0, 2, 1, 3, 2, 0, 3, 1, 0, 1, 3, 0, 1)
KINDS = (BF16, BF16, F32)
LAG = 99
contract_rows = (((0,), (0,)), ((), ()))
contract_cols = (((1,), (1,)), ((), ()))


def swap(value, dim):
    flips = DIMS[dim]
    if len(flips) == 1:
        axis, flip = flips[0]
        return lax.ppermute(value, axis, [(i, i ^ flip) for i in range(SIZES[axis])])
    pairs = []
    for x in range(4):
        for zl in range(4):
            for c, (axis, flip) in enumerate(flips):
                to = (x ^ flip, zl) if axis == "x" else (x, zl ^ flip)
                pairs.append(((x * 4 + zl) * 2 + c, (to[0] * 4 + to[1]) * 2 + c))
    return lax.ppermute(value, ("x", "zl", "c"), pairs)


def take(value, names, dim, index):
    return lax.index_in_dim(value, index, names.index(dim), keepdims=False)


def pick(value, names, dim, index):
    return lax.dynamic_index_in_dim(value, index, names.index(dim), keepdims=False)


def local_backward(total, size):
    gate, up, back = total[:, :size], total[:, size : 2 * size], total[:, 2 * size :]
    sig = jax.nn.sigmoid(gate)
    silu = gate * sig
    hidden = (silu * up).astype(BF16)
    d_up = (back * silu).astype(BF16)
    d_gate = (back * up * sig * (1.0 + gate * (1.0 - sig))).astype(BF16)
    return jnp.concatenate([d_gate, d_up, hidden], axis=1)


def merge(pair, order):
    names = "".join(n for n in ROW if n in order)
    return jnp.stack(pair, axis=names.index(order[-1]))


def on_device(inputs, out_grad, gate_weight, up_weight, down_weight):
    rows, width = inputs.shape
    x, zl, core = lax.axis_index("x"), lax.axis_index("zl"), lax.axis_index("c")
    on_x, on_z = ((x & 1) ^ (x >> 1), x >> 1), zl & 1
    bits = (on_x[0], on_x[1], on_z), (on_x[1], on_z, on_x[0])
    bit = {n: jnp.where(core == 0, bits[0][k], bits[1][k]) for k, n in enumerate("HFE")}
    bit["G"] = jnp.zeros_like(x)
    differs = {n: bits[0][k] != bits[1][k] for k, n in enumerate("HFE")}

    def reorder(value, names, dim, turn):
        first, second = (take(value, names, dim, k) for k in (0, 1))
        return jnp.stack([jnp.where(turn, second, first), jnp.where(turn, first, second)], axis=names.index(dim))

    def from_core(value, names):
        for dim in "FE":
            value = reorder(value, names, dim, differs[dim])
        return value

    def gather(value, order, names):
        for dim in order:
            other = swap(value, dim)
            if dim == "H":
                other = from_core(other, names)
            names = "".join(n for n in COL if n in names or n == dim)
            mine = bit[dim] == 0
            value = jnp.stack([jnp.where(mine, value, other), jnp.where(mine, other, value)], axis=names.index(dim))
        return value

    both = gather(jnp.concatenate([inputs, out_grad], axis=1), "G", "")
    x_cols = gather(both[..., :width], "EFH", "G")
    g_cols = gather(both[..., width:], "FEH", "G")
    x_flat, g_flat = (v.reshape(16 * rows, width) for v in (x_cols, g_cols))
    x_turned = x_flat.T
    def forward(cols, first, index, start, size):
        xh, gh = (take(v, ROW, first, index).reshape(8 * rows, width) for v in cols)
        gate = jnp.dot(xh, gate_weight[:, start : start + size], preferred_element_type=F32)
        up = jnp.dot(xh, up_weight[:, start : start + size], preferred_element_type=F32)
        back = lax.dot_general(gh, down_weight[start : start + size], contract_cols, preferred_element_type=F32)
        return jnp.concatenate([gate, up, back], axis=1).reshape(2, 2, 2, rows, 3 * size)

    starts = [sum(c[0] for c in CHUNKS[:i]) for i in range(len(CHUNKS))]
    state = [None] * len(CHUNKS)
    step = [0] * len(CHUNKS)
    last = None
    due = {}
    grads = [None] * len(CHUNKS)
    acc_input = 0.0

    def tie(value, *more):
        nonlocal last
        if last is not None:
            value, last, more = lax.optimization_barrier((value, last, more))
        last = value
        return (value, *more) if more else value

    def after(*values):
        nonlocal last
        values, last = lax.optimization_barrier((values, last))
        return values

    def send(value, dim, kind=BF16):
        return swap(tie(value.astype(kind)), dim)

    def split(value, size):
        return value[:, :size], value[:, size : 2 * size], value[:, 2 * size :]

    def input_products(i):
        size, _, up = CHUNKS[i]
        columns = slice(starts[i], starts[i] + size)
        d_gate, d_up, _ = split(merge(state[i], "D" + up).reshape(16 * rows, 3 * size), size)
        part = lax.dot_general(d_gate, gate_weight[:, columns], contract_cols, preferred_element_type=F32)
        return part + lax.dot_general(d_up, up_weight[:, columns], contract_cols, preferred_element_type=F32)

    def weight_products(i):
        size, _, up = CHUNKS[i]
        d_gate, d_up, hidden = split(merge(state[i], "D" + up).reshape(16 * rows, 3 * size), size)
        return (
            with_layout_constraint(jnp.dot(x_turned, d_gate, preferred_element_type=F32).astype(BF16), Layout(major_to_minor=(0, 1))),
            with_layout_constraint(jnp.dot(x_turned, d_up, preferred_element_type=F32).astype(BF16), Layout(major_to_minor=(0, 1))),
            lax.dot_general(hidden, g_flat, contract_rows, preferred_element_type=F32).astype(BF16),
        )

    for n, i in enumerate(ORDER):
        size, down, up = CHUNKS[i]
        s = step[i]
        names = "".join(n for n in ROW if n not in down[:s])
        if s == 0:
            dim = down[0]
            state[i] = [send(forward((x_cols, g_cols), dim, 1, starts[i], size), dim)]
        elif s < 3:
            dim = down[s]
            state[i][-1], *cols = after(state[i][-1], x_cols, g_cols)
            if s == 1:
                state[i] = [forward(cols, down[0], 0, starts[i], size), *state[i]]
            other = send(sum(take(p, names, dim, 1).astype(F32) for p in state[i]), dim, KINDS[s])
            state[i] = [take(p, names, dim, 0) for p in state[i]] + [other]
        elif s == 3:
            state[i][-1], = after(state[i][-1])
            value = sum(p.astype(F32) for p in state[i]).reshape(2 * rows, 3 * size)
            state[i] = (value, send(value, "D"))
        else:
            state[i] = (state[i][0], *after(*state[i][1:]))
            if s == 4:
                value = local_backward(state[i][0] + state[i][1].astype(F32), size)
                value = value.reshape(2, rows, 3 * size)
            else:
                value = merge(state[i], "D" + up[: s - 4])
            if due and min(due) <= n:
                j = due.pop(min(due))
                value, acc_input, grads[j] = tie(value, acc_input + input_products(j), weight_products(j))
            else:
                value = tie(value)
            state[i] = (value, swap(value, up[s - 4]))
        step[i] += 1
        if step[i] == 7:
            due[n + LAG] = i

    def scatter(value, order, names):
        for dim in order:
            kept = pick(value, names, dim, bit[dim])
            other = swap(pick(value, names, dim, 1 - bit[dim]), dim)
            names = names.replace(dim, "")
            value = kept + (from_core(other, names) if dim == "H" else other)
        return value

    for j in due.values():
        acc_input = acc_input + input_products(j)
    acc_input = tie(acc_input.reshape(2, 2, 2, 2, rows, width))
    acc_input = scatter(acc_input, "H", COL)
    left = scatter(acc_input[..., : width // 2], "FE", "FEG")
    right = scatter(acc_input[..., width // 2 :], "EF", "FEG")
    acc_input = scatter(jnp.concatenate([left, right], axis=-1), "G", "G")
    for j in due.values():
        state[j], last = lax.optimization_barrier((state[j], last))
        grads[j] = weight_products(j)
    gate_grads, up_grads, down_grads = zip(*grads)
    return (
        acc_input.astype(BF16),
        with_layout_constraint(jnp.concatenate(gate_grads, axis=1), Layout(major_to_minor=(0, 1))),
        with_layout_constraint(jnp.concatenate(up_grads, axis=1), Layout(major_to_minor=(0, 1))),
        jnp.concatenate(down_grads, axis=0),
    )


def solution(mesh):
    fine = Mesh(mesh.devices.reshape(4, 4, 4, 2, 2), ("x", "zl", "y", "zh", "c"))
    row, col = ("x", "zl"), ("y", "zh", "c")
    in_specs = (P(col, row), P(col, row), P(row, col), P(row, col), P(col, row))
    out_specs = (P(col, row), P(row, col), P(row, col), P(col, row))
    return jax.shard_map(
        on_device, mesh=fine, in_specs=in_specs, out_specs=out_specs, check_vma=False
    )
```

```python
import jax
import jax.numpy as jnp
from jax import lax
from jax.experimental.layout import Layout, with_layout_constraint
from jax.sharding import Mesh, PartitionSpec as P

BF16, F32 = jnp.bfloat16, jnp.float32
DIMS = {
    "P": (("x", 1), ("x", 3)), "Q": (("x", 3), ("zl", 1)), "R": (("zl", 1), ("x", 1)), "D": (("zl", 2),),
    "E": (("y", 1),), "F": (("y", 3),), "G": (("zh", 1),), "H": (("c", 1),),
}
SIZES = {"x": 4, "zl": 4, "y": 4, "zh": 2, "c": 2}
ROW, COL = "PQRD", "HFEG"
CHUNKS = ((512, 'QRP', 'PRQ'), (384, 'QPR', 'PQR'), (384, 'PRQ', 'PRQ'), (512, 'PRQ', 'QRP'))
ORDER = (2, 3, 0, 1, 2, 3, 2, 0, 3, 1, 2, 0, 3, 1, 2, 0, 2, 1, 3, 2, 0, 3, 1, 0, 1, 3, 0, 1)
KINDS = (BF16, BF16, F32)
LAG = 99
contract_rows = (((0,), (0,)), ((), ()))
contract_cols = (((1,), (1,)), ((), ()))


def swap(value, dim):
    flips = DIMS[dim]
    if len(flips) == 1:
        axis, flip = flips[0]
        return lax.ppermute(value, axis, [(i, i ^ flip) for i in range(SIZES[axis])])
    pairs = []
    for x in range(4):
        for zl in range(4):
            for c, (axis, flip) in enumerate(flips):
                to = (x ^ flip, zl) if axis == "x" else (x, zl ^ flip)
                pairs.append(((x * 4 + zl) * 2 + c, (to[0] * 4 + to[1]) * 2 + c))
    return lax.ppermute(value, ("x", "zl", "c"), pairs)


def take(value, names, dim, index):
    return lax.index_in_dim(value, index, names.index(dim), keepdims=False)


def pick(value, names, dim, index):
    return lax.dynamic_index_in_dim(value, index, names.index(dim), keepdims=False)


def local_backward(total, size):
    gate, up, back = total[:, :size], total[:, size : 2 * size], total[:, 2 * size :]
    sig = jax.nn.sigmoid(gate)
    silu = gate * sig
    hidden = (silu * up).astype(BF16)
    d_up = (back * silu).astype(BF16)
    d_gate = (back * up * sig * (1.0 + gate * (1.0 - sig))).astype(BF16)
    return jnp.concatenate([d_gate, d_up, hidden], axis=1)


def merge(pair, order):
    names = "".join(n for n in ROW if n in order)
    return jnp.stack(pair, axis=names.index(order[-1]))


def on_device(inputs, out_grad, gate_weight, up_weight, down_weight):
    rows, width = inputs.shape
    x, zl, core = lax.axis_index("x"), lax.axis_index("zl"), lax.axis_index("c")
    on_x, on_z = ((x & 1) ^ (x >> 1), x >> 1), zl & 1
    bits = (on_x[0], on_x[1], on_z), (on_x[1], on_z, on_x[0])
    bit = {n: jnp.where(core == 0, bits[0][k], bits[1][k]) for k, n in enumerate("HFE")}
    bit["G"] = jnp.zeros_like(x)
    differs = {n: bits[0][k] != bits[1][k] for k, n in enumerate("HFE")}

    def reorder(value, names, dim, turn):
        first, second = (take(value, names, dim, k) for k in (0, 1))
        return jnp.stack([jnp.where(turn, second, first), jnp.where(turn, first, second)], axis=names.index(dim))

    def from_core(value, names):
        for dim in "FE":
            value = reorder(value, names, dim, differs[dim])
        return value

    def gather(value, order, names):
        for dim in order:
            other = swap(value, dim)
            if dim == "H":
                other = from_core(other, names)
            names = "".join(n for n in COL if n in names or n == dim)
            mine = bit[dim] == 0
            value = jnp.stack([jnp.where(mine, value, other), jnp.where(mine, other, value)], axis=names.index(dim))
        return value

    both = gather(jnp.concatenate([inputs, out_grad], axis=1), "G", "")
    x_cols = gather(both[..., :width], "EFH", "G")
    g_cols = gather(both[..., width:], "FEH", "G")
    x_flat, g_flat = (v.reshape(16 * rows, width) for v in (x_cols, g_cols))
    x_turned = x_flat.T
    def forward(cols, first, index, start, size):
        xh, gh = (take(v, ROW, first, index).reshape(8 * rows, width) for v in cols)
        gate = jnp.dot(xh, gate_weight[:, start : start + size], preferred_element_type=F32)
        up = jnp.dot(xh, up_weight[:, start : start + size], preferred_element_type=F32)
        back = lax.dot_general(gh, down_weight[start : start + size], contract_cols, preferred_element_type=F32)
        return jnp.concatenate([gate, up, back], axis=1).reshape(2, 2, 2, rows, 3 * size)

    starts = [sum(c[0] for c in CHUNKS[:i]) for i in range(len(CHUNKS))]
    state = [None] * len(CHUNKS)
    step = [0] * len(CHUNKS)
    last = None
    due = {}
    grads = [None] * len(CHUNKS)
    acc_input = 0.0

    def tie(value, *more):
        nonlocal last
        if last is not None:
            value, last, more = lax.optimization_barrier((value, last, more))
        last = value
        return (value, *more) if more else value

    def after(*values):
        nonlocal last
        values, last = lax.optimization_barrier((values, last))
        return values

    def send(value, dim, kind=BF16):
        return swap(tie(value.astype(kind)), dim)

    def split(value, size):
        return value[:, :size], value[:, size : 2 * size], value[:, 2 * size :]

    def input_products(i):
        size, _, up = CHUNKS[i]
        columns = slice(starts[i], starts[i] + size)
        d_gate, d_up, _ = split(merge(state[i], "D" + up).reshape(16 * rows, 3 * size), size)
        part = lax.dot_general(d_gate, gate_weight[:, columns], contract_cols, preferred_element_type=F32)
        return part + lax.dot_general(d_up, up_weight[:, columns], contract_cols, preferred_element_type=F32)

    def weight_products(i):
        size, _, up = CHUNKS[i]
        d_gate, d_up, hidden = split(merge(state[i], "D" + up).reshape(16 * rows, 3 * size), size)
        return (
            with_layout_constraint(jnp.dot(x_turned, d_gate, preferred_element_type=F32).astype(BF16), Layout(major_to_minor=(0, 1))),
            with_layout_constraint(jnp.dot(x_turned, d_up, preferred_element_type=F32).astype(BF16), Layout(major_to_minor=(0, 1))),
            lax.dot_general(hidden, g_flat, contract_rows, preferred_element_type=F32).astype(BF16),
        )

    for n, i in enumerate(ORDER):
        size, down, up = CHUNKS[i]
        s = step[i]
        names = "".join(n for n in ROW if n not in down[:s])
        if s == 0:
            dim = down[0]
            state[i] = [send(forward((x_cols, g_cols), dim, 1, starts[i], size), dim)]
        elif s < 3:
            dim = down[s]
            state[i][-1], *cols = after(state[i][-1], x_cols, g_cols)
            if s == 1:
                state[i] = [forward(cols, down[0], 0, starts[i], size), *state[i]]
            other = send(sum(take(p, names, dim, 1).astype(F32) for p in state[i]), dim, KINDS[s])
            state[i] = [take(p, names, dim, 0) for p in state[i]] + [other]
        elif s == 3:
            state[i][-1], = after(state[i][-1])
            value = sum(p.astype(F32) for p in state[i]).reshape(2 * rows, 3 * size)
            state[i] = (value, send(value, "D"))
        else:
            if s == 4:
                state[i] = (state[i][0], *after(*state[i][1:]))
            if s == 4:
                value = local_backward(state[i][0] + state[i][1].astype(F32), size)
                value = value.reshape(2, rows, 3 * size)
            else:
                value = merge(state[i], "D" + up[: s - 4])
            if due and min(due) <= n:
                j = due.pop(min(due))
                value, acc_input, grads[j] = tie(value, acc_input + input_products(j), weight_products(j))
            else:
                value = tie(value)
            state[i] = (value, swap(value, up[s - 4]))
        step[i] += 1
        if step[i] == 7:
            due[n + LAG] = i

    def scatter(value, order, names):
        for dim in order:
            kept = pick(value, names, dim, bit[dim])
            other = swap(pick(value, names, dim, 1 - bit[dim]), dim)
            names = names.replace(dim, "")
            value = kept + (from_core(other, names) if dim == "H" else other)
        return value

    for j in due.values():
        acc_input = acc_input + input_products(j)
    acc_input = tie(acc_input.reshape(2, 2, 2, 2, rows, width))
    acc_input = scatter(acc_input, "H", COL)
    left = scatter(acc_input[..., : width // 2], "FE", "FEG")
    right = scatter(acc_input[..., width // 2 :], "EF", "FEG")
    acc_input = scatter(jnp.concatenate([left, right], axis=-1), "G", "G")
    for j in due.values():
        state[j], last = lax.optimization_barrier((state[j], last))
        grads[j] = weight_products(j)
    gate_grads, up_grads, down_grads = zip(*grads)
    return (
        acc_input.astype(BF16),
        with_layout_constraint(jnp.concatenate(gate_grads, axis=1), Layout(major_to_minor=(0, 1))),
        with_layout_constraint(jnp.concatenate(up_grads, axis=1), Layout(major_to_minor=(0, 1))),
        jnp.concatenate(down_grads, axis=0),
    )


def solution(mesh):
    fine = Mesh(mesh.devices.reshape(4, 4, 4, 2, 2), ("x", "zl", "y", "zh", "c"))
    row, col = ("x", "zl"), ("y", "zh", "c")
    in_specs = (P(col, row), P(col, row), P(row, col), P(row, col), P(col, row))
    out_specs = (P(col, row), P(row, col), P(row, col), P(col, row))
    return jax.shard_map(
        on_device, mesh=fine, in_specs=in_specs, out_specs=out_specs, check_vma=False
    )
```
